32 devices in a mesh: groups: 2 (over y), expert: 4 (over z), fsdp: 4 (over x, core).
Axes of the slice: x: 2, y: 2, z: 4, core: 2. Of those that a mesh axis runs over, the one named last changes fastest.
Arguments:
- tokens: bfloat16 [8192, 2048], P(('groups', 'expert', 'fsdp')), parts along dimension 0, may hold values from -6 to 6
- cotangent: bfloat16 [8192, 2048], P(('groups', 'expert', 'fsdp')), parts along dimension 0, may hold values from -6 to 6
- expert_ids: int32 [8192], P(('groups', 'expert', 'fsdp')), parts along dimension 0, may hold values from 0 to 3, as said below
- gate_weight: bfloat16 [4, 2048, 768], P('expert', 'fsdp'), may hold values from -0.125 to 0.125
- up_weight: bfloat16 [4, 2048, 768], P('expert', 'fsdp'), may hold values from -0.125 to 0.125
- down_weight: bfloat16 [4, 768, 2048], P('expert', None, 'fsdp'), may hold values from -0.21875 to 0.21875
Outputs:
- layer_output: bfloat16 [8192, 2048], P(('groups', 'expert', 'fsdp')), parts along dimension 0
- grad_tokens: bfloat16 [8192, 2048], P(('groups', 'expert', 'fsdp')), parts along dimension 0
- gate_grad: bfloat16 [8, 2048, 768], P(('groups', 'expert'), 'fsdp'), parts along dimension 0
- up_grad: bfloat16 [8, 2048, 768], P(('groups', 'expert'), 'fsdp'), parts along dimension 0
- down_grad: bfloat16 [8, 768, 2048], P(('groups', 'expert'), None, 'fsdp'), parts along dimension 0
The draws below stay inside these ranges and needn't reach their ends.
There are 2 independent parts, one for each index of `groups`. The reference program is written for one: setup_inputs(seed, part) draws one part's arguments, and reference() takes and returns one part's arrays. A program takes and returns all parts, laid end to end along the dimension named above; an argument that names none is the same for every part. Nothing has to cross between parts.
Inputs may be any that keep to these rules, and one draw needn't show every extreme that they name: `expert_ids`: among the 256 tokens of one device (an aligned block of 256), no expert is named more than 128 times; in every draw one expert is named exactly 128 times in every such block.
All inputs are finite; a program needn't handle non-finite values.
Results may differ from the reference program's by a relative error of at most 0.009.
Values may be sent and summed in bfloat16 or wider, within the bound.
A program may use at most 128 MiB of HBM per device.

```python
import jax
import jax.numpy as jnp
from jax import lax

D = 2048
H = 768
TOK_DEV = 256
EXPERTS = 4
CAP = 128
TOKENS = 4096
N_EXPERT = 4
N_FSDP = 4


def draw_expert_ids(key, part):
    key = jax.random.fold_in(key, 7)
    block_count = TOKENS // TOK_DEV
    slot_count = EXPERTS * CAP
    subkeys = jax.random.split(key, 4)
    hot_expert = jax.random.randint(subkeys[0], (), 0, EXPERTS, dtype=jnp.int32)
    popularity = jax.random.randint(subkeys[1], (EXPERTS,), 0, 4, dtype=jnp.int32)
    slot_numbers = jnp.arange(slot_count, dtype=jnp.int32)
    slot_owner = slot_numbers // CAP
    first_slot = slot_numbers % CAP == 0
    edge_owner = (slot_owner == 0) | (slot_owner == EXPERTS - 1)
    forced = first_slot & edge_owner
    jitter = jax.random.randint(subkeys[2], (block_count, slot_count), 0, 65536, dtype=jnp.int32)
    ranking = popularity[slot_owner][None, :] * 65536 + jitter
    ranking = jnp.where(slot_owner[None, :] == hot_expert, 5 * 65536, ranking)
    ranking = jnp.where(forced[None, :], 6 * 65536, ranking)
    ranking = ranking * slot_count + (slot_count - 1 - slot_numbers)[None, :]
    chosen = lax.top_k(ranking, TOK_DEV)[1]
    picked = (chosen // CAP).astype(jnp.int32)
    shuffle = jax.vmap(jax.random.permutation)(jax.random.split(subkeys[3], block_count), picked)
    return shuffle.reshape(TOKENS).astype(jnp.int32)


def level_of(stream_key, dims, cuts, least, high):
    def one(position, parts):
        steps = jax.random.uniform(jax.random.fold_in(jax.random.fold_in(stream_key, 6), position), (parts,), jnp.float32, least / len(cuts), high / len(cuts))
        return jnp.repeat(jnp.exp(steps), dims[position] // parts).reshape((-1,) + (1,) * (len(dims) - position - 1))

    gain = one(*cuts[0])
    for cut in cuts[1:]:
        gain = gain * one(*cut)
    return gain


def scatter_about(rng, dims, deviation, limit, cuts=(), held_as=jnp.bfloat16):
    level = level_of(rng, dims, cuts, -0.22, 0.18) if cuts else 1.0
    result = jax.random.normal(rng, dims, jnp.float32) * deviation * level
    return jnp.minimum(jnp.maximum(result, -limit), limit).astype(held_as)


def setup_inputs(seed: int = 0, part: int = 0) -> dict:
    keys = jax.random.split(jax.random.key(seed), 7)
    part_keys = jax.random.split(jax.random.fold_in(keys[6], part), 7)
    tokens = scatter_about(part_keys[0], (TOKENS, D), 1.0, 6.0, ((0, 16),))
    cotangent = scatter_about(part_keys[1], (TOKENS, D), 1.0, 6.0, ((0, 16),))
    expert_ids = draw_expert_ids(jax.random.fold_in(jax.random.fold_in(keys[6], part), 71), part)
    gate_weight = scatter_about(keys[3], (EXPERTS, D, H), D ** -0.5, 0.125, ((0, 4), (1, 4)))
    up_weight = scatter_about(keys[4], (EXPERTS, D, H), D ** -0.5, 0.125, ((0, 4), (1, 4)))
    down_weight = scatter_about(keys[5], (EXPERTS, H, D), H ** -0.5, 0.21875, ((0, 4), (2, 4)))
    return dict(tokens=tokens, cotangent=cotangent, expert_ids=expert_ids, gate_weight=gate_weight, up_weight=up_weight, down_weight=down_weight)


loss_scale = 0.015625


def slot_positions(expert_ids, expert_count, capacity):
    onehot_table = (expert_ids[:, None] == jnp.arange(expert_count, dtype=jnp.int32)[None, :]).astype(jnp.int32)
    earlier = jnp.cumsum(onehot_table, axis=0) - onehot_table
    rank_within = jnp.sum(earlier * onehot_table, axis=1)
    return (expert_ids * capacity + rank_within).astype(jnp.int32)


def contract_last(left, right):
    return lax.dot_general(left, right, (((1,), (1,)), ((), ())), preferred_element_type=jnp.float32)


def contract_first(left, right):
    return lax.dot_general(left, right, (((0,), (0,)), ((), ())), preferred_element_type=jnp.float32)


def forward_rows(recv_rows, w_gate, w_up, w_down):
    gate_act = jnp.dot(recv_rows, w_gate, preferred_element_type=jnp.float32)
    up_act = jnp.dot(recv_rows, w_up, preferred_element_type=jnp.float32)
    sigmoid_gate = jax.nn.sigmoid(gate_act)
    hidden = (gate_act * sigmoid_gate * up_act).astype(jnp.bfloat16)
    out_rows = jnp.dot(hidden, w_down, preferred_element_type=jnp.float32).astype(jnp.bfloat16)
    return gate_act, up_act, hidden, out_rows


def backward_rows(grad_out, gate_act, up_act, w_gate, w_up, w_down):
    grad_hidden = contract_last(grad_out, w_down)
    sigmoid_gate = jax.nn.sigmoid(gate_act)
    grad_gate = (grad_hidden * up_act * sigmoid_gate * (1.0 + gate_act * (1.0 - sigmoid_gate))).astype(jnp.bfloat16)
    grad_up = (grad_hidden * gate_act * sigmoid_gate).astype(jnp.bfloat16)
    grad_rows = (contract_last(grad_gate, w_gate) + contract_last(grad_up, w_up)).astype(jnp.bfloat16)
    return grad_gate, grad_up, grad_rows


def owner_block(recv_rows, grad_out, w_gate, w_up, w_down):
    gate_act, up_act, hidden, out_rows = forward_rows(recv_rows, w_gate, w_up, w_down)
    grad_gate, grad_up, grad_rows = backward_rows(grad_out, gate_act, up_act, w_gate, w_up, w_down)
    both_grads = jnp.concatenate([grad_gate, grad_up], axis=1)
    first_terms = contract_first(recv_rows, both_grads)
    second_terms = contract_first(grad_out, hidden)
    terms = (jnp.concatenate([first_terms, second_terms], axis=1) * loss_scale).astype(jnp.bfloat16)
    return out_rows, grad_rows, terms


def reference(tokens, cotangent, expert_ids, gate_weight, up_weight, down_weight):
    device_count = N_EXPERT * N_FSDP
    slot_count = EXPERTS * CAP
    slot_index = jax.vmap(lambda ids: slot_positions(ids, EXPERTS, CAP))(expert_ids.reshape(device_count, TOK_DEV))

    def pack_slots(device_rows, places):
        return jnp.zeros((slot_count, D), jnp.bfloat16).at[places].set(device_rows)

    def arrange(array):
        buffer = jax.vmap(pack_slots)(array.reshape(device_count, TOK_DEV, D), slot_index)
        buffer = buffer.reshape(N_EXPERT, N_FSDP, EXPERTS, CAP, D)
        return jnp.transpose(buffer, (2, 1, 0, 3, 4)).reshape(EXPERTS, N_FSDP, N_EXPERT * CAP, D)

    rows_all = arrange(tokens)
    grads_all = arrange(cotangent)

    def expert_work(expert_items):
        rows_e, grads_e, w_gate, w_up, w_down = expert_items

        def share_work(share_items):
            return owner_block(share_items[0], share_items[1], w_gate, w_up, w_down)

        out_rows, grad_rows, terms = lax.map(share_work, (rows_e, grads_e))
        summed = jnp.sum(terms.astype(jnp.float32), axis=0).astype(jnp.bfloat16)
        return out_rows, grad_rows, summed

    out_all, grad_all, summed = lax.map(expert_work, (rows_all, grads_all, gate_weight, up_weight, down_weight))

    def restore(buffer):
        buffer = buffer.reshape(EXPERTS, N_FSDP, N_EXPERT, CAP, D)
        buffer = jnp.transpose(buffer, (2, 1, 0, 3, 4)).reshape(device_count, slot_count, D)
        return jax.vmap(lambda slots_rows, places: slots_rows[places])(buffer, slot_index).reshape(TOKENS, D)

    gate_grad = summed[:, :, :H]
    up_grad = summed[:, :, H:2 * H]
    down_grad = jnp.transpose(summed[:, :, 2 * H:], (0, 2, 1))
    return restore(out_all), restore(grad_all), gate_grad, up_grad, down_grad
```

```python
import jax
import jax.numpy as jnp
from jax import lax
from jax.sharding import PartitionSpec as P

loss_scale = 0.015625
bf16 = jnp.bfloat16
f32 = jnp.float32


def dot_dims(left, right, l, r):
    return lax.dot_general(left, right, (((l,), (r,)), ((), ())), preferred_element_type=f32)


def shift(x, axis, k):
    n = lax.axis_size(axis)
    return lax.ppermute(x, axis, [(i, (i + k) % n) for i in range(n)])


def swap_core(x):
    n = lax.axis_size("fsdp")
    return lax.ppermute(x, "fsdp", [(i, i ^ 1) for i in range(n)])


def gather_weight(w, dim):
    n = lax.axis_size("fsdp")
    me = lax.axis_index("fsdp")
    core = me % 2
    size = w.shape[dim]
    shape = list(w.shape)
    shape[dim] = size * n
    full = jnp.zeros(shape, w.dtype)
    for j in range(n // 2):
        mine = w if j == 0 else shift(w, "fsdp", 2 * j)
        other = swap_core(mine)
        owner = (me - 2 * j + n) % n
        full = lax.dynamic_update_slice_in_dim(full, mine, owner * size, dim)
        full = lax.dynamic_update_slice_in_dim(full, other, (owner + 1 - 2 * core) * size, dim)
    return full


def scatter_sum(part):
    n = lax.axis_size("fsdp")
    me = lax.axis_index("fsdp")
    core = me % 2
    cols = part.shape[1]
    blocks = part.reshape(n // 2, 2, part.shape[0] // n, cols)
    keep = lax.dynamic_index_in_dim(blocks, core, 1, keepdims=False)
    give = lax.dynamic_index_in_dim(blocks, 1 - core, 1, keepdims=False)
    chip = keep.astype(f32) + swap_core(give).astype(f32)
    x = me // 2
    half = n // 2
    total = lax.dynamic_index_in_dim(chip, x, 0, keepdims=False)
    chip16 = chip.astype(bf16)
    for j in range(1, half):
        out = lax.dynamic_index_in_dim(chip16, (x + j) % half, 0, keepdims=False)
        total = total + shift(out, "fsdp", 2 * j).astype(f32)
    return total.astype(bf16)


def body(tokens, cotangent, expert_ids, gate_weight, up_weight, down_weight):
    rows, features = tokens.shape
    owners = lax.axis_size("expert")
    me = lax.axis_index("expert")
    cap = 2 * rows // owners
    w_gate = gather_weight(gate_weight[0], 0)
    w_up = gather_weight(up_weight[0], 0)
    w_down = gather_weight(down_weight[0], 1)
    onehot = (expert_ids[:, None] == jnp.arange(owners, dtype=jnp.int32)[None, :]).astype(bf16)
    t = jnp.arange(rows, dtype=jnp.int32)
    before = (t[None, :] < t[:, None]).astype(bf16)
    earlier = jnp.dot(before, onehot, preferred_element_type=f32)
    rank = jnp.sum(earlier * onehot.astype(f32), axis=1).astype(jnp.int32)
    slot = ((expert_ids - me + owners) % owners) * cap + rank
    order = [k for k in range(owners) if k % 2 == 0] + [k for k in range(owners) if k % 2]
    half = owners // 2
    chunks = (order[:half], order[half:])

    def select(ks):
        want = jnp.concatenate([k * cap + jnp.arange(cap, dtype=jnp.int32) for k in ks])
        return (want[:, None] == slot[None, :]).astype(bf16)

    picks = [select(ks) for ks in chunks]
    recv = []
    for ks, pick in zip(chunks, picks):
        got = []
        for array in (tokens, cotangent):
            sent = jnp.dot(pick, array, preferred_element_type=f32).astype(bf16)
            got.append(
                jnp.concatenate(
                    [
                        sent[i * cap : (i + 1) * cap]
                        if k == 0
                        else shift(sent[i * cap : (i + 1) * cap], "expert", k)
                        for i, k in enumerate(ks)
                    ]
                )
            )
        recv.append(got)
    hiddens, gates, ups = [], [], []
    home_out, home_grad = [], []
    for ks, (x, g) in zip(chunks, recv):
        gate_act = jnp.dot(x, w_gate, preferred_element_type=f32)
        up_act = jnp.dot(x, w_up, preferred_element_type=f32)
        s = jax.nn.sigmoid(gate_act)
        hidden = (gate_act * s * up_act).astype(bf16)
        out = jnp.dot(hidden, w_down, preferred_element_type=f32).astype(bf16)
        grad_hidden = dot_dims(g, w_down, 1, 1)
        grad_gate = (grad_hidden * up_act * s * (1.0 + gate_act * (1.0 - s))).astype(bf16)
        grad_up = (grad_hidden * gate_act * s).astype(bf16)
        grad = (dot_dims(grad_gate, w_gate, 1, 1) + dot_dims(grad_up, w_up, 1, 1)).astype(bf16)
        hiddens.append(hidden)
        gates.append(grad_gate)
        ups.append(grad_up)
        for result, home in ((out, home_out), (grad, home_grad)):
            home.extend(
                result[i * cap : (i + 1) * cap]
                if k == 0
                else shift(result[i * cap : (i + 1) * cap], "expert", -k)
                for i, k in enumerate(ks)
            )
    x_all = jnp.concatenate([recv[0][0], recv[1][0]])
    g_all = jnp.concatenate([recv[0][1], recv[1][1]])
    gate_part = (dot_dims(x_all, jnp.concatenate(gates), 0, 0) * loss_scale).astype(bf16)
    up_part = (dot_dims(x_all, jnp.concatenate(ups), 0, 0) * loss_scale).astype(bf16)
    down_part = (dot_dims(g_all, jnp.concatenate(hiddens), 0, 0) * loss_scale).astype(bf16)
    gate_grad = scatter_sum(gate_part)[None]
    up_grad = scatter_sum(up_part)[None]
    down_grad = jnp.transpose(scatter_sum(down_part))[None]
    pick_all = jnp.concatenate(picks)
    layer_output = dot_dims(pick_all, jnp.concatenate(home_out), 0, 0).astype(bf16)
    grad_tokens = dot_dims(pick_all, jnp.concatenate(home_grad), 0, 0).astype(bf16)
    return (layer_output, grad_tokens, gate_grad, up_grad, down_grad)


def solution(mesh):
    rows = P(("groups", "expert", "fsdp"), None)
    return jax.shard_map(
        body,
        mesh=mesh,
        in_specs=(
            rows,
            rows,
            P(("groups", "expert", "fsdp")),
            P("expert", "fsdp", None),
            P("expert", "fsdp", None),
            P("expert", None, "fsdp"),
        ),
        out_specs=(
            rows,
            rows,
            P(("groups", "expert"), "fsdp", None),
            P(("groups", "expert"), "fsdp", None),
            P(("groups", "expert"), None, "fsdp"),
        ),
        check_vma=False,
    )
```

```python
import functools

import jax
import jax.numpy as jnp
from jax import lax
from jax.experimental import pallas as pl
from jax.experimental.pallas import tpu as pltpu
from jax.sharding import PartitionSpec as P

loss_scale = 0.015625
bf16 = jnp.bfloat16
f32 = jnp.float32
MESH = pl.DeviceIdType.MESH
TILE = 256


def dot_dims(left, right, l, r):
    return lax.dot_general(left, right, (((l,), (r,)), ((), ())), preferred_element_type=f32)


def tile_at(i, size):
    return pl.ds(pl.multiple_of(i * size, size), size)


def layer_kernel(
    owners, shards, cap, order,
    sx, sg, wg, wu, wd,
    ho, hg, gate_out, up_out, down_out,
    rx, rg, wgf, wuf, wdf, hid, gg, gu, out, grad, part, from_core, from_x,
    wx_send, wx_recv, wc_send, wc_recv, w_loc,
    in_send, in_recv, in_loc, out_send, out_recv, out_loc,
    rc_send, rc_recv, rx_send, rx_recv,
):
    me = lax.axis_index("expert")
    shard = lax.axis_index("fsdp")
    chips = shards // 2
    chip = shard // 2
    core = lax.rem(shard, 2)
    peer = 2 * chip + 1 - core
    features = rx.shape[1]
    hidden = hid.shape[1]
    size = features // shards
    half = owners // 2
    rows = half * cap

    def at_chip(j):
        return 2 * lax.rem(chip + j, chips) + core

    def remote(src, dst, send, recv, axis, index):
        return pltpu.make_async_remote_copy(
            src_ref=src, dst_ref=dst, send_sem=send, recv_sem=recv,
            device_id={axis: index}, device_id_type=MESH,
        )

    barrier = pltpu.get_barrier_semaphore()
    for k in range(1, owners):
        pl.semaphore_signal(barrier, inc=1, device_id={"expert": lax.rem(me + k, owners)}, device_id_type=MESH)
    for j in range(1, chips):
        pl.semaphore_signal(barrier, inc=1, device_id={"fsdp": at_chip(j)}, device_id_type=MESH)
    pl.semaphore_signal(barrier, inc=1, device_id={"fsdp": peer}, device_id_type=MESH)
    pl.semaphore_wait(barrier, owners - 1 + chips)

    weights = ((wg, wgf, 0), (wu, wuf, 0), (wd, wdf, 1))

    def slab(full, dim, index):
        where = tile_at(index, size)
        return full.at[where, :] if dim == 0 else full.at[:, where]

    over_x, over_core, own = [], [], []
    for w, (src, full, dim) in enumerate(weights):
        over_x.append([
            remote(src, slab(full, dim, shard), wx_send.at[w, j], wx_recv.at[w, j], "fsdp", at_chip(j))
            for j in range(1, chips)
        ])
        first = remote(src, slab(full, dim, shard), wc_send.at[w, 0], wc_recv.at[w, 0], "fsdp", peer)
        over_core.append([first])
        own.append(pltpu.make_async_copy(src, slab(full, dim, shard), w_loc.at[w]))

    def send_in(a, i):
        src, dst = ((sx, rx), (sg, rg))[a]
        where = pl.ds(i * cap, cap)
        if order[i] == 0:
            return pltpu.make_async_copy(src.at[where, :], dst.at[where, :], in_loc.at[a])
        return remote(
            src.at[where, :], dst.at[where, :], in_send.at[a, i], in_recv.at[a, i],
            "expert", lax.rem(me + order[i], owners),
        )

    ins = [[send_in(a, i) for i in range(owners)] for a in range(2)]

    def start_in(c, a):
        for i in range(c * half, (c + 1) * half):
            ins[a][i].start()

    def sent_in(c, a):
        for i in range(c * half, (c + 1) * half):
            if order[i]:
                ins[a][i].wait_send()

    def got_in(c, a):
        for i in range(c * half, (c + 1) * half):
            if order[i]:
                ins[a][i].wait_recv()
            else:
                ins[a][i].wait()

    def forward(w):
        src, full, dim = weights[w]
        for j in range(1, chips):
            over_x[w][j - 1].wait_recv()
            block = slab(full, dim, 2 * lax.rem(chip + chips - j, chips) + core)
            copy = remote(block, block, wc_send.at[w, j], wc_recv.at[w, j], "fsdp", peer)
            copy.start()
            over_core[w].append(copy)

    def got_weight(w):
        own[w].wait()
        for copy in over_core[w]:
            copy.wait_recv()

    for w in range(3):
        for copy in over_x[w]:
            copy.start()
    start_in(0, 0)
    start_in(0, 1)
    for w in range(3):
        over_core[w][0].start()
        own[w].start()
    forward(0)
    sent_in(0, 0)
    start_in(1, 0)
    forward(1)
    sent_in(0, 1)
    start_in(1, 1)
    forward(2)

    def send_out(a, i):
        src, dst = ((out, ho), (grad, hg))[a]
        where = pl.ds(i * cap, cap)
        if order[i] == 0:
            return pltpu.make_async_copy(src.at[where, :], dst.at[where, :], out_loc.at[a])
        return remote(
            src.at[where, :], dst.at[where, :], out_send.at[a, i], out_recv.at[a, i],
            "expert", lax.rem(me + owners - order[i], owners),
        )

    outs = [[send_out(a, i) for i in range(owners)] for a in range(2)]

    def compute(c):
        these = pl.ds(c * rows, rows)
        got_in(c, 0)
        got_in(c, 1)
        if c == 0:
            for w in range(3):
                got_weight(w)

        @pl.loop(0, hidden // TILE)
        def _(t):
            where = tile_at(t, TILE)
            gate_act = jnp.dot(rx[these, :], wgf[:, where], preferred_element_type=f32)
            up_act = jnp.dot(rx[these, :], wuf[:, where], preferred_element_type=f32)
            grad_hidden = dot_dims(rg[these, :], wdf[where, :], 1, 1)
            s = jax.nn.sigmoid(gate_act)
            gated = gate_act * s
            hid[these, where] = (gated * up_act).astype(bf16)
            gg[these, where] = (grad_hidden * up_act * s * (1.0 + gate_act * (1.0 - s))).astype(bf16)
            gu[these, where] = (grad_hidden * gated).astype(bf16)

        @pl.loop(0, features // TILE)
        def _(t):
            where = tile_at(t, TILE)
            out[these, where] = jnp.dot(hid[these, :], wdf[:, where], preferred_element_type=f32).astype(bf16)

        for i in range(c * half, (c + 1) * half):
            outs[0][i].start()

        @pl.loop(0, features // TILE)
        def _(t):
            where = tile_at(t, TILE)
            grad[these, where] = (
                dot_dims(gg[these, :], wgf[where, :], 1, 1) + dot_dims(gu[these, :], wuf[where, :], 1, 1)
            ).astype(bf16)

        for i in range(c * half, (c + 1) * half):
            outs[1][i].start()

    compute(0)
    compute(1)

    def block_partial(index):
        @pl.loop(0, size // TILE)
        def _(t):
            where = pl.ds(pl.multiple_of(index * size + t * TILE, TILE), TILE)
            x = rx[:, where]
            part[where, 0:hidden] = (dot_dims(x, gg[...], 0, 0) * loss_scale).astype(bf16)
            part[where, hidden : 2 * hidden] = (dot_dims(x, gu[...], 0, 0) * loss_scale).astype(bf16)
            part[where, 2 * hidden : 3 * hidden] = (dot_dims(rg[:, where], hid[...], 0, 0) * loss_scale).astype(bf16)

    to_core = []
    for j in range(1, chips + 1):
        slot = j % chips
        index = 2 * lax.rem(chip + j, chips) + 1 - core
        block_partial(index)
        copy = remote(
            part.at[tile_at(index, size), :], from_core.at[slot], rc_send.at[slot], rc_recv.at[slot], "fsdp", peer
        )
        copy.start()
        to_core.append(copy)
    step = 32
    to_x = []
    for j in range(1, chips):
        index = at_chip(j)
        block_partial(index)
        to_core[j - 1].wait_recv()

        @pl.loop(0, size // step)
        def _(t):
            here = pl.ds(pl.multiple_of(index * size + t * step, step), step)
            there = tile_at(t, step)
            part[here, :] = (part[here, :].astype(f32) + from_core[j, there, :].astype(f32)).astype(bf16)

        copy = remote(
            part.at[tile_at(index, size), :], from_x.at[j - 1], rx_send.at[j], rx_recv.at[j], "fsdp", index
        )
        copy.start()
        to_x.append(copy)
    block_partial(shard)
    to_core[chips - 1].wait_recv()
    for copy in to_x:
        copy.wait_recv()

    @pl.loop(0, size // step)
    def _(t):
        here = pl.ds(pl.multiple_of(shard * size + t * step, step), step)
        there = tile_at(t, step)
        total = part[here, :].astype(f32) + from_core[0, there, :].astype(f32)
        for j in range(1, chips):
            total = total + from_x[j - 1, there, :].astype(f32)
        total = total.astype(bf16)
        gate_out[there, :] = total[:, 0:hidden]
        up_out[there, :] = total[:, hidden : 2 * hidden]
        down_out[there, :] = total[:, 2 * hidden : 3 * hidden]

    for w in range(3):
        for copy in over_x[w] + over_core[w]:
            copy.wait_send()
    for a in range(2):
        sent_in(1, a)
    for copy in to_core + to_x:
        copy.wait_send()
    for a in range(2):
        for copy in outs[a]:
            copy.wait()


def body(tokens, cotangent, expert_ids, gate_weight, up_weight, down_weight):
    rows, features = tokens.shape
    hidden = gate_weight.shape[2]
    owners = lax.axis_size("expert")
    shards = lax.axis_size("fsdp")
    chips = shards // 2
    me = lax.axis_index("expert")
    cap = 2 * rows // owners
    slots = owners * cap
    size = features // shards
    order = [k for k in range(owners) if k % 2 == 0] + [k for k in range(owners) if k % 2]
    onehot = (expert_ids[:, None] == jnp.arange(owners, dtype=jnp.int32)[None, :]).astype(bf16)
    t = jnp.arange(rows, dtype=jnp.int32)
    before = (t[None, :] < t[:, None]).astype(bf16)
    earlier = jnp.dot(before, onehot, preferred_element_type=f32)
    rank = jnp.sum(earlier * onehot.astype(f32), axis=1).astype(jnp.int32)
    k = (expert_ids - me + owners) % owners
    place = k // 2 + (k % 2) * (owners // 2)
    slot = place * cap + rank
    pick = (jnp.arange(slots, dtype=jnp.int32)[:, None] == slot[None, :]).astype(bf16)
    sx = jnp.dot(pick, tokens, preferred_element_type=f32).astype(bf16)
    sg = jnp.dot(pick, cotangent, preferred_element_type=f32).astype(bf16)

    dma = pltpu.SemaphoreType.DMA
    anywhere = pl.BlockSpec(memory_space=pl.ANY)
    vmem = pl.BlockSpec(memory_space=pltpu.VMEM)
    row_shape = jax.ShapeDtypeStruct((slots, features), bf16)
    sum_shape = jax.ShapeDtypeStruct((size, hidden), bf16)
    ho, hg, gate_grad, up_grad, down_grad = pl.pallas_call(
        functools.partial(layer_kernel, owners, shards, cap, order),
        out_shape=(row_shape, row_shape, sum_shape, sum_shape, sum_shape),
        in_specs=[anywhere] * 5,
        out_specs=(anywhere, anywhere, vmem, vmem, vmem),
        scratch_shapes=[
            pltpu.VMEM((slots, features), bf16),
            pltpu.VMEM((slots, features), bf16),
            pltpu.VMEM((features, hidden), bf16),
            pltpu.VMEM((features, hidden), bf16),
            pltpu.VMEM((hidden, features), bf16),
            pltpu.VMEM((slots, hidden), bf16),
            pltpu.VMEM((slots, hidden), bf16),
            pltpu.VMEM((slots, hidden), bf16),
            pltpu.VMEM((slots, features), bf16),
            pltpu.VMEM((slots, features), bf16),
            pltpu.VMEM((features, 3 * hidden), bf16),
            pltpu.VMEM((chips, size, 3 * hidden), bf16),
            pltpu.VMEM((chips - 1, size, 3 * hidden), bf16),
            dma((3, chips)), dma((3, chips)), dma((3, chips)), dma((3, chips)), dma((3,)),
            dma((2, owners)), dma((2, owners)), dma((2,)),
            dma((2, owners)), dma((2, owners)), dma((2,)),
            dma((chips,)), dma((chips,)), dma((chips,)), dma((chips,)),
        ],
        compiler_params=pltpu.CompilerParams(
            collective_id=0, has_side_effects=True, vmem_limit_bytes=58 * 1024 * 1024
        ),
        cost_estimate=pl.CostEstimate(
            flops=18 * slots * features * hidden, bytes_accessed=40 * 1024 * 1024, transcendentals=slots * hidden
        ),
    )(sx, sg, gate_weight[0], up_weight[0], down_weight[0])
    layer_output = dot_dims(pick, ho, 0, 0).astype(bf16)
    grad_tokens = dot_dims(pick, hg, 0, 0).astype(bf16)
    return (layer_output, grad_tokens, gate_grad[None], up_grad[None], jnp.transpose(down_grad)[None])


def solution(mesh):
    rows = P(("groups", "expert", "fsdp"), None)
    return jax.shard_map(
        body,
        mesh=mesh,
        in_specs=(
            rows,
            rows,
            P(("groups", "expert", "fsdp")),
            P("expert", "fsdp", None),
            P("expert", "fsdp", None),
            P("expert", None, "fsdp"),
        ),
        out_specs=(
            rows,
            rows,
            P(("groups", "expert"), "fsdp", None),
            P(("groups", "expert"), "fsdp", None),
            P(("groups", "expert"), None, "fsdp"),
        ),
        check_vma=False,
    )
```

```python
import functools

import jax
import jax.numpy as jnp
from jax import lax
from jax.experimental import pallas as pl
from jax.experimental.pallas import tpu as pltpu
from jax.sharding import PartitionSpec as P

loss_scale = 0.015625
bf16 = jnp.bfloat16
f32 = jnp.float32
MESH = pl.DeviceIdType.MESH
TILE = 256


def dot_dims(left, right, l, r):
    return lax.dot_general(left, right, (((l,), (r,)), ((), ())), preferred_element_type=f32)


def tile_at(i, size):
    return pl.ds(pl.multiple_of(i * size, size), size)


def layer_kernel(
    owners, shards, cap, order,
    pick, tok, cot, wg, wu, wd,
    ho, hg, gate_out, up_out, down_out,
    sx, sg, rx, rg, wgf, wuf, wdf, hid, gg, gu, out, grad, part, from_core, from_x,
    wx_send, wx_recv, wc_send, wc_recv, w_loc,
    in_send, in_recv, out_send, out_recv, out_loc,
    rc_send, rc_recv, rx_send, rx_recv,
):
    me = lax.axis_index("expert")
    shard = lax.axis_index("fsdp")
    chips = shards // 2
    chip = shard // 2
    core = lax.rem(shard, 2)
    peer = 2 * chip + 1 - core
    features = rx.shape[1]
    hidden = hid.shape[1]
    size = features // shards
    half = owners // 2
    rows = half * cap

    def at_chip(j):
        return 2 * lax.rem(chip + j, chips) + core

    def remote(src, dst, send, recv, axis, index):
        return pltpu.make_async_remote_copy(
            src_ref=src, dst_ref=dst, send_sem=send, recv_sem=recv,
            device_id={axis: index}, device_id_type=MESH,
        )

    barrier = pltpu.get_barrier_semaphore()
    for k in range(1, owners):
        pl.semaphore_signal(barrier, inc=1, device_id={"expert": lax.rem(me + k, owners)}, device_id_type=MESH)
    for j in range(1, chips):
        pl.semaphore_signal(barrier, inc=1, device_id={"fsdp": at_chip(j)}, device_id_type=MESH)
    pl.semaphore_signal(barrier, inc=1, device_id={"fsdp": peer}, device_id_type=MESH)
    pl.semaphore_wait(barrier, owners - 1 + chips)

    weights = ((wg, wgf, 0), (wu, wuf, 0), (wd, wdf, 1))

    def slab(full, dim, index):
        where = tile_at(index, size)
        return full.at[where, :] if dim == 0 else full.at[:, where]

    over_x, over_core, own = [], [], []
    for w, (src, full, dim) in enumerate(weights):
        over_x.append([
            remote(src, slab(full, dim, shard), wx_send.at[w, j], wx_recv.at[w, j], "fsdp", at_chip(j))
            for j in range(1, chips)
        ])
        first = remote(src, slab(full, dim, shard), wc_send.at[w, 0], wc_recv.at[w, 0], "fsdp", peer)
        over_core.append([first])
        own.append(pltpu.make_async_copy(src, slab(full, dim, shard), w_loc.at[w]))

    def send_in(a, i):
        src, dst = ((sx, rx), (sg, rg))[a]
        where = pl.ds(i * cap, cap)
        if order[i] == 0:
            return None
        return remote(
            src.at[where, :], dst.at[where, :], in_send.at[a, i], in_recv.at[a, i],
            "expert", lax.rem(me + order[i], owners),
        )

    ins = [[send_in(a, i) for i in range(owners)] for a in range(2)]

    def start_in(c, a):
        rows_in, sent, kept = ((tok, sx, rx), (cot, sg, rg))[a]
        low = cap if c == 0 else 0
        picked = pick[c * rows : (c + 1) * rows, :]

        @pl.loop(0, features // TILE)
        def _(t):
            where = tile_at(t, TILE)
            block = jnp.dot(picked, rows_in[:, where], preferred_element_type=f32).astype(bf16)
            if c == 0:
                kept[0:cap, where] = block[0:cap]
            sent[c * rows + low : (c + 1) * rows, where] = block[low:]

        for i in range(c * half, (c + 1) * half):
            if order[i]:
                ins[a][i].start()

    def sent_in(c, a):
        for i in range(c * half, (c + 1) * half):
            if order[i]:
                ins[a][i].wait_send()

    def got_in(c, a):
        for i in range(c * half, (c + 1) * half):
            if order[i]:
                ins[a][i].wait_recv()

    def forward(w):
        src, full, dim = weights[w]
        for j in range(1, chips):
            over_x[w][j - 1].wait_recv()
            block = slab(full, dim, 2 * lax.rem(chip + chips - j, chips) + core)
            copy = remote(block, block, wc_send.at[w, j], wc_recv.at[w, j], "fsdp", peer)
            copy.start()
            over_core[w].append(copy)

    def got_weight(w):
        own[w].wait()
        for copy in over_core[w]:
            copy.wait_recv()

    for w in range(3):
        for copy in over_x[w]:
            copy.start()
    start_in(0, 0)
    start_in(0, 1)
    for w in range(3):
        over_core[w][0].start()
        own[w].start()
    forward(0)
    sent_in(0, 0)
    start_in(1, 0)
    forward(1)
    sent_in(0, 1)
    start_in(1, 1)
    forward(2)

    def send_out(a, i):
        src, dst = ((out, ho), (grad, hg))[a]
        where = pl.ds(i * cap, cap)
        if order[i] == 0:
            return pltpu.make_async_copy(src.at[where, :], dst.at[where, :], out_loc.at[a])
        return remote(
            src.at[where, :], dst.at[where, :], out_send.at[a, i], out_recv.at[a, i],
            "expert", lax.rem(me + owners - order[i], owners),
        )

    outs = [[send_out(a, i) for i in range(owners)] for a in range(2)]

    def start_out(c, a):
        for i in range(c * half, (c + 1) * half):
            outs[a][i].start()

    def compute(c):
        these = pl.ds(c * rows, rows)
        @pl.loop(0, hidden // TILE)
        def _(t):
            where = tile_at(t, TILE)
            gate_act = jnp.dot(rx[these, :], wgf[:, where], preferred_element_type=f32)
            up_act = jnp.dot(rx[these, :], wuf[:, where], preferred_element_type=f32)
            grad_hidden = dot_dims(rg[these, :], wdf[where, :], 1, 1)
            s = jax.nn.sigmoid(gate_act)
            gated = gate_act * s
            hid[these, where] = (gated * up_act).astype(bf16)
            gg[these, where] = (grad_hidden * up_act * s * (1.0 + gate_act * (1.0 - s))).astype(bf16)
            gu[these, where] = (grad_hidden * gated).astype(bf16)

        @pl.loop(0, features // TILE)
        def _(t):
            where = tile_at(t, TILE)
            out[these, where] = jnp.dot(hid[these, :], wdf[:, where], preferred_element_type=f32).astype(bf16)

        if c == 1:
            start_out(c, 0)

        @pl.loop(0, features // TILE)
        def _(t):
            where = tile_at(t, TILE)
            grad[these, where] = (
                dot_dims(gg[these, :], wgf[where, :], 1, 1) + dot_dims(gu[these, :], wuf[where, :], 1, 1)
            ).astype(bf16)

        if c == 1:
            start_out(c, 1)

    got_in(0, 0)
    got_in(0, 1)
    for w in range(3):
        got_weight(w)
    compute(0)
    got_in(1, 0)
    start_out(0, 0)
    got_in(1, 1)
    start_out(0, 1)
    compute(1)

    def block_partial(index):
        @pl.loop(0, size // TILE)
        def _(t):
            where = pl.ds(pl.multiple_of(index * size + t * TILE, TILE), TILE)
            x = rx[:, where]
            part[where, 0:hidden] = (dot_dims(x, gg[...], 0, 0) * loss_scale).astype(bf16)
            part[where, hidden : 2 * hidden] = (dot_dims(x, gu[...], 0, 0) * loss_scale).astype(bf16)
            part[where, 2 * hidden : 3 * hidden] = (dot_dims(rg[:, where], hid[...], 0, 0) * loss_scale).astype(bf16)

    to_core = []
    for j in range(1, chips + 1):
        slot = j % chips
        index = 2 * lax.rem(chip + j, chips) + 1 - core
        block_partial(index)
        copy = remote(
            part.at[tile_at(index, size), :], from_core.at[slot], rc_send.at[slot], rc_recv.at[slot], "fsdp", peer
        )
        copy.start()
        to_core.append(copy)
    step = 32
    to_x = []
    for j in range(1, chips):
        index = at_chip(j)
        block_partial(index)
        to_core[j - 1].wait_recv()

        @pl.loop(0, size // step)
        def _(t):
            here = pl.ds(pl.multiple_of(index * size + t * step, step), step)
            there = tile_at(t, step)
            part[here, :] = (part[here, :].astype(f32) + from_core[j, there, :].astype(f32)).astype(bf16)

        copy = remote(
            part.at[tile_at(index, size), :], from_x.at[j - 1], rx_send.at[j], rx_recv.at[j], "fsdp", index
        )
        copy.start()
        to_x.append(copy)
    block_partial(shard)
    to_core[chips - 1].wait_recv()
    for copy in to_x:
        copy.wait_recv()

    @pl.loop(0, size // step)
    def _(t):
        here = pl.ds(pl.multiple_of(shard * size + t * step, step), step)
        there = tile_at(t, step)
        total = part[here, :].astype(f32) + from_core[0, there, :].astype(f32)
        for j in range(1, chips):
            total = total + from_x[j - 1, there, :].astype(f32)
        total = total.astype(bf16)
        gate_out[there, :] = total[:, 0:hidden]
        up_out[there, :] = total[:, hidden : 2 * hidden]
        down_out[there, :] = total[:, 2 * hidden : 3 * hidden]

    for w in range(3):
        for copy in over_x[w] + over_core[w]:
            copy.wait_send()
    for a in range(2):
        sent_in(1, a)
    for copy in to_core + to_x:
        copy.wait_send()
    for a in range(2):
        for copy in outs[a]:
            copy.wait()


def body(tokens, cotangent, expert_ids, gate_weight, up_weight, down_weight):
    rows, features = tokens.shape
    hidden = gate_weight.shape[2]
    owners = lax.axis_size("expert")
    shards = lax.axis_size("fsdp")
    chips = shards // 2
    me = lax.axis_index("expert")
    cap = 2 * rows // owners
    slots = owners * cap
    size = features // shards
    order = [k for k in range(owners) if k % 2 == 0] + [k for k in range(owners) if k % 2]
    onehot = (expert_ids[:, None] == jnp.arange(owners, dtype=jnp.int32)[None, :]).astype(bf16)
    t = jnp.arange(rows, dtype=jnp.int32)
    before = (t[None, :] < t[:, None]).astype(bf16)
    earlier = jnp.dot(before, onehot, preferred_element_type=f32)
    rank = jnp.sum(earlier * onehot.astype(f32), axis=1).astype(jnp.int32)
    k = (expert_ids - me + owners) % owners
    place = k // 2 + (k % 2) * (owners // 2)
    slot = place * cap + rank
    pick = (jnp.arange(slots, dtype=jnp.int32)[:, None] == slot[None, :]).astype(bf16)

    dma = pltpu.SemaphoreType.DMA
    anywhere = pl.BlockSpec(memory_space=pl.ANY)
    vmem = pl.BlockSpec(memory_space=pltpu.VMEM)
    row_shape = jax.ShapeDtypeStruct((slots, features), bf16)
    sum_shape = jax.ShapeDtypeStruct((size, hidden), bf16)
    ho, hg, gate_grad, up_grad, down_grad = pl.pallas_call(
        functools.partial(layer_kernel, owners, shards, cap, order),
        out_shape=(row_shape, row_shape, sum_shape, sum_shape, sum_shape),
        in_specs=[vmem] * 3 + [anywhere] * 3,
        out_specs=(anywhere, anywhere, vmem, vmem, vmem),
        scratch_shapes=[
            pltpu.VMEM((slots, features), bf16),
            pltpu.VMEM((slots, features), bf16),
            pltpu.VMEM((slots, features), bf16),
            pltpu.VMEM((slots, features), bf16),
            pltpu.VMEM((features, hidden), bf16),
            pltpu.VMEM((features, hidden), bf16),
            pltpu.VMEM((hidden, features), bf16),
            pltpu.VMEM((slots, hidden), bf16),
            pltpu.VMEM((slots, hidden), bf16),
            pltpu.VMEM((slots, hidden), bf16),
            pltpu.VMEM((slots, features), bf16),
            pltpu.VMEM((slots, features), bf16),
            pltpu.VMEM((features, 3 * hidden), bf16),
            pltpu.VMEM((chips, size, 3 * hidden), bf16),
            pltpu.VMEM((chips - 1, size, 3 * hidden), bf16),
            dma((3, chips)), dma((3, chips)), dma((3, chips)), dma((3, chips)), dma((3,)),
            dma((2, owners)), dma((2, owners)),
            dma((2, owners)), dma((2, owners)), dma((2,)),
            dma((chips,)), dma((chips,)), dma((chips,)), dma((chips,)),
        ],
        compiler_params=pltpu.CompilerParams(
            collective_id=0, has_side_effects=True, vmem_limit_bytes=58 * 1024 * 1024
        ),
        cost_estimate=pl.CostEstimate(
            flops=18 * slots * features * hidden, bytes_accessed=40 * 1024 * 1024, transcendentals=slots * hidden
        ),
    )(pick, tokens, cotangent, gate_weight[0], up_weight[0], down_weight[0])
    layer_output = dot_dims(pick, ho, 0, 0).astype(bf16)
    grad_tokens = dot_dims(pick, hg, 0, 0).astype(bf16)
    return (layer_output, grad_tokens, gate_grad[None], up_grad[None], jnp.transpose(down_grad)[None])


def solution(mesh):
    rows = P(("groups", "expert", "fsdp"), None)
    return jax.shard_map(
        body,
        mesh=mesh,
        in_specs=(
            rows,
            rows,
            P(("groups", "expert", "fsdp")),
            P("expert", "fsdp", None),
            P("expert", "fsdp", None),
            P("expert", None, "fsdp"),
        ),
        out_specs=(
            rows,
            rows,
            P(("groups", "expert"), "fsdp", None),
            P(("groups", "expert"), "fsdp", None),
            P(("groups", "expert"), None, "fsdp"),
        ),
        check_vma=False,
    )
```

```python
import functools

import jax
import jax.numpy as jnp
from jax import lax
from jax.experimental import pallas as pl
from jax.experimental.pallas import tpu as pltpu
from jax.sharding import PartitionSpec as P

loss_scale = 0.015625
bf16 = jnp.bfloat16
f32 = jnp.float32
MESH = pl.DeviceIdType.MESH
TILE = 256


def dot_dims(left, right, l, r):
    return lax.dot_general(left, right, (((l,), (r,)), ((), ())), preferred_element_type=f32)


def tile_at(i, size):
    return pl.ds(pl.multiple_of(i * size, size), size)


def layer_kernel(
    owners, shards, cap, order,
    pick, tok, cot, wg, wu, wd,
    ho, hg, gate_out, up_out, down_out,
    sx, sg, rx, rg, wgf, wuf, wdf, hid, gg, gu, out, grad, part, from_core, from_x,
    wx_send, wx_recv, wc_send, wc_recv, w_loc,
    in_send, in_recv, out_send, out_recv, out_loc,
    rc_send, rc_recv, rx_send, rx_recv,
):
    me = lax.axis_index("expert")
    shard = lax.axis_index("fsdp")
    chips = shards // 2
    chip = shard // 2
    core = lax.rem(shard, 2)
    peer = 2 * chip + 1 - core
    features = rx.shape[1]
    hidden = hid.shape[1]
    size = features // shards
    half = owners // 2
    rows = half * cap

    def at_chip(j):
        return 2 * lax.rem(chip + j, chips) + core

    def remote(src, dst, send, recv, axis, index):
        return pltpu.make_async_remote_copy(
            src_ref=src, dst_ref=dst, send_sem=send, recv_sem=recv,
            device_id={axis: index}, device_id_type=MESH,
        )

    barrier = pltpu.get_barrier_semaphore()
    for k in range(1, owners):
        pl.semaphore_signal(barrier, inc=1, device_id={"expert": lax.rem(me + k, owners)}, device_id_type=MESH)
    for j in range(1, chips):
        pl.semaphore_signal(barrier, inc=1, device_id={"fsdp": at_chip(j)}, device_id_type=MESH)
    pl.semaphore_signal(barrier, inc=1, device_id={"fsdp": peer}, device_id_type=MESH)
    pl.semaphore_wait(barrier, owners - 1 + chips)

    weights = ((wg, wgf, 0), (wu, wuf, 0), (wd, wdf, 1))

    def slab(full, dim, index):
        where = tile_at(index, size)
        return full.at[where, :] if dim == 0 else full.at[:, where]

    over_x, over_core, own = [], [], []
    for w, (src, full, dim) in enumerate(weights):
        over_x.append([
            remote(src, slab(full, dim, shard), wx_send.at[w, j], wx_recv.at[w, j], "fsdp", at_chip(j))
            for j in range(1, chips)
        ])
        first = remote(src, slab(full, dim, shard), wc_send.at[w, 0], wc_recv.at[w, 0], "fsdp", peer)
        over_core.append([first])
        own.append(pltpu.make_async_copy(src, slab(full, dim, shard), w_loc.at[w]))

    def send_in(a, i):
        src, dst = ((sx, rx), (sg, rg))[a]
        where = pl.ds(i * cap, cap)
        if order[i] == 0:
            return None
        return remote(
            src.at[where, :], dst.at[where, :], in_send.at[a, i], in_recv.at[a, i],
            "expert", lax.rem(me + order[i], owners),
        )

    ins = [[send_in(a, i) for i in range(owners)] for a in range(2)]

    def start_far_first(copies, c, flip):
        mine = [copy for copy in copies[c * half : (c + 1) * half] if copy is not None]

        @pl.when(lax.rem(me + flip, 2) == 0)
        def _():
            for copy in mine:
                copy.start()

        @pl.when(lax.rem(me + flip, 2) == 1)
        def _():
            for copy in reversed(mine):
                copy.start()

    def start_in(c, a):
        rows_in, sent, kept = ((tok, sx, rx), (cot, sg, rg))[a]
        low = cap if c == 0 else 0
        picked = pick[c * rows : (c + 1) * rows, :]

        @pl.loop(0, features // TILE)
        def _(t):
            where = tile_at(t, TILE)
            block = jnp.dot(picked, rows_in[:, where], preferred_element_type=f32).astype(bf16)
            if c == 0:
                kept[0:cap, where] = block[0:cap]
            sent[c * rows + low : (c + 1) * rows, where] = block[low:]

        start_far_first(ins[a], c, 1)

    def sent_in(c, a):
        for i in range(c * half, (c + 1) * half):
            if order[i]:
                ins[a][i].wait_send()

    def got_in(c, a):
        for i in range(c * half, (c + 1) * half):
            if order[i]:
                ins[a][i].wait_recv()

    def forward(w):
        src, full, dim = weights[w]
        for j in range(1, chips):
            over_x[w][j - 1].wait_recv()
            block = slab(full, dim, 2 * lax.rem(chip + chips - j, chips) + core)
            copy = remote(block, block, wc_send.at[w, j], wc_recv.at[w, j], "fsdp", peer)
            copy.start()
            over_core[w].append(copy)

    def got_weight(w):
        own[w].wait()
        for copy in over_core[w]:
            copy.wait_recv()

    for w in range(3):
        for copy in over_x[w]:
            copy.start()
    start_in(0, 0)
    start_in(0, 1)
    for w in range(3):
        over_core[w][0].start()
        own[w].start()
    forward(0)
    sent_in(0, 0)
    start_in(1, 0)
    forward(1)
    sent_in(0, 1)
    start_in(1, 1)
    forward(2)

    def send_out(a, i):
        src, dst = ((out, ho), (grad, hg))[a]
        where = pl.ds(i * cap, cap)
        if order[i] == 0:
            return pltpu.make_async_copy(src.at[where, :], dst.at[where, :], out_loc.at[a])
        return remote(
            src.at[where, :], dst.at[where, :], out_send.at[a, i], out_recv.at[a, i],
            "expert", lax.rem(me + owners - order[i], owners),
        )

    outs = [[send_out(a, i) for i in range(owners)] for a in range(2)]

    def start_out(c, a):
        start_far_first(outs[a], c, 0)

    def compute(c):
        these = pl.ds(c * rows, rows)
        @pl.loop(0, hidden // TILE)
        def _(t):
            where = tile_at(t, TILE)
            gate_act = jnp.dot(rx[these, :], wgf[:, where], preferred_element_type=f32)
            up_act = jnp.dot(rx[these, :], wuf[:, where], preferred_element_type=f32)
            grad_hidden = dot_dims(rg[these, :], wdf[where, :], 1, 1)
            s = jax.nn.sigmoid(gate_act)
            gated = gate_act * s
            hid[these, where] = (gated * up_act).astype(bf16)
            gg[these, where] = (grad_hidden * up_act * s * (1.0 + gate_act * (1.0 - s))).astype(bf16)
            gu[these, where] = (grad_hidden * gated).astype(bf16)

        @pl.loop(0, features // TILE)
        def _(t):
            where = tile_at(t, TILE)
            out[these, where] = jnp.dot(hid[these, :], wdf[:, where], preferred_element_type=f32).astype(bf16)

        if c == 1:
            start_out(c, 0)

        @pl.loop(0, features // TILE)
        def _(t):
            where = tile_at(t, TILE)
            grad[these, where] = (
                dot_dims(gg[these, :], wgf[where, :], 1, 1) + dot_dims(gu[these, :], wuf[where, :], 1, 1)
            ).astype(bf16)

        if c == 1:
            start_out(c, 1)

    got_in(0, 0)
    got_in(0, 1)
    for w in range(3):
        got_weight(w)
    compute(0)
    got_in(1, 0)
    start_out(0, 0)
    got_in(1, 1)
    start_out(0, 1)
    compute(1)

    def block_partial(index):
        @pl.loop(0, size // TILE)
        def _(t):
            where = pl.ds(pl.multiple_of(index * size + t * TILE, TILE), TILE)
            x = rx[:, where]
            part[where, 0:hidden] = (dot_dims(x, gg[...], 0, 0) * loss_scale).astype(bf16)
            part[where, hidden : 2 * hidden] = (dot_dims(x, gu[...], 0, 0) * loss_scale).astype(bf16)
            part[where, 2 * hidden : 3 * hidden] = (dot_dims(rg[:, where], hid[...], 0, 0) * loss_scale).astype(bf16)

    to_core = []
    for j in range(1, chips + 1):
        slot = j % chips
        index = 2 * lax.rem(chip + j, chips) + 1 - core
        block_partial(index)
        copy = remote(
            part.at[tile_at(index, size), :], from_core.at[slot], rc_send.at[slot], rc_recv.at[slot], "fsdp", peer
        )
        copy.start()
        to_core.append(copy)
    step = 32
    to_x = []
    for j in range(1, chips):
        index = at_chip(j)
        block_partial(index)
        to_core[j - 1].wait_recv()

        @pl.loop(0, size // step)
        def _(t):
            here = pl.ds(pl.multiple_of(index * size + t * step, step), step)
            there = tile_at(t, step)
            part[here, :] = (part[here, :].astype(f32) + from_core[j, there, :].astype(f32)).astype(bf16)

        copy = remote(
            part.at[tile_at(index, size), :], from_x.at[j - 1], rx_send.at[j], rx_recv.at[j], "fsdp", index
        )
        copy.start()
        to_x.append(copy)
    block_partial(shard)
    to_core[chips - 1].wait_recv()
    for copy in to_x:
        copy.wait_recv()

    @pl.loop(0, size // step)
    def _(t):
        here = pl.ds(pl.multiple_of(shard * size + t * step, step), step)
        there = tile_at(t, step)
        total = part[here, :].astype(f32) + from_core[0, there, :].astype(f32)
        for j in range(1, chips):
            total = total + from_x[j - 1, there, :].astype(f32)
        total = total.astype(bf16)
        gate_out[there, :] = total[:, 0:hidden]
        up_out[there, :] = total[:, hidden : 2 * hidden]
        down_out[there, :] = total[:, 2 * hidden : 3 * hidden]

    for w in range(3):
        for copy in over_x[w] + over_core[w]:
            copy.wait_send()
    for a in range(2):
        sent_in(1, a)
    for copy in to_core + to_x:
        copy.wait_send()
    for a in range(2):
        for copy in outs[a]:
            copy.wait()


def body(tokens, cotangent, expert_ids, gate_weight, up_weight, down_weight):
    rows, features = tokens.shape
    hidden = gate_weight.shape[2]
    owners = lax.axis_size("expert")
    shards = lax.axis_size("fsdp")
    chips = shards // 2
    me = lax.axis_index("expert")
    cap = 2 * rows // owners
    slots = owners * cap
    size = features // shards
    order = [k for k in range(owners) if k % 2 == 0] + [k for k in range(owners) if k % 2]
    onehot = (expert_ids[:, None] == jnp.arange(owners, dtype=jnp.int32)[None, :]).astype(bf16)
    t = jnp.arange(rows, dtype=jnp.int32)
    before = (t[None, :] < t[:, None]).astype(bf16)
    earlier = jnp.dot(before, onehot, preferred_element_type=f32)
    rank = jnp.sum(earlier * onehot.astype(f32), axis=1).astype(jnp.int32)
    k = (expert_ids - me + owners) % owners
    place = k // 2 + (k % 2) * (owners // 2)
    slot = place * cap + rank
    pick = (jnp.arange(slots, dtype=jnp.int32)[:, None] == slot[None, :]).astype(bf16)

    dma = pltpu.SemaphoreType.DMA
    anywhere = pl.BlockSpec(memory_space=pl.ANY)
    vmem = pl.BlockSpec(memory_space=pltpu.VMEM)
    row_shape = jax.ShapeDtypeStruct((slots, features), bf16)
    sum_shape = jax.ShapeDtypeStruct((size, hidden), bf16)
    ho, hg, gate_grad, up_grad, down_grad = pl.pallas_call(
        functools.partial(layer_kernel, owners, shards, cap, order),
        out_shape=(row_shape, row_shape, sum_shape, sum_shape, sum_shape),
        in_specs=[vmem] * 3 + [anywhere] * 3,
        out_specs=(anywhere, anywhere, vmem, vmem, vmem),
        scratch_shapes=[
            pltpu.VMEM((slots, features), bf16),
            pltpu.VMEM((slots, features), bf16),
            pltpu.VMEM((slots, features), bf16),
            pltpu.VMEM((slots, features), bf16),
            pltpu.VMEM((features, hidden), bf16),
            pltpu.VMEM((features, hidden), bf16),
            pltpu.VMEM((hidden, features), bf16),
            pltpu.VMEM((slots, hidden), bf16),
            pltpu.VMEM((slots, hidden), bf16),
            pltpu.VMEM((slots, hidden), bf16),
            pltpu.VMEM((slots, features), bf16),
            pltpu.VMEM((slots, features), bf16),
            pltpu.VMEM((features, 3 * hidden), bf16),
            pltpu.VMEM((chips, size, 3 * hidden), bf16),
            pltpu.VMEM((chips - 1, size, 3 * hidden), bf16),
            dma((3, chips)), dma((3, chips)), dma((3, chips)), dma((3, chips)), dma((3,)),
            dma((2, owners)), dma((2, owners)),
            dma((2, owners)), dma((2, owners)), dma((2,)),
            dma((chips,)), dma((chips,)), dma((chips,)), dma((chips,)),
        ],
        compiler_params=pltpu.CompilerParams(
            collective_id=0, has_side_effects=True, vmem_limit_bytes=58 * 1024 * 1024
        ),
        cost_estimate=pl.CostEstimate(
            flops=18 * slots * features * hidden, bytes_accessed=40 * 1024 * 1024, transcendentals=slots * hidden
        ),
    )(pick, tokens, cotangent, gate_weight[0], up_weight[0], down_weight[0])
    layer_output = dot_dims(pick, ho, 0, 0).astype(bf16)
    grad_tokens = dot_dims(pick, hg, 0, 0).astype(bf16)
    return (layer_output, grad_tokens, gate_grad[None], up_grad[None], jnp.transpose(down_grad)[None])


def solution(mesh):
    rows = P(("groups", "expert", "fsdp"), None)
    return jax.shard_map(
        body,
        mesh=mesh,
        in_specs=(
            rows,
            rows,
            P(("groups", "expert", "fsdp")),
            P("expert", "fsdp", None),
            P("expert", "fsdp", None),
            P("expert", None, "fsdp"),
        ),
        out_specs=(
            rows,
            rows,
            P(("groups", "expert"), "fsdp", None),
            P(("groups", "expert"), "fsdp", None),
            P(("groups", "expert"), None, "fsdp"),
        ),
        check_vma=False,
    )
```
